32 devices in a mesh: seq: 4 (over y, core), wide: 8 (over z, x).
Axes of the slice: x: 2, y: 2, z: 4, core: 2. Of those that a mesh axis runs over, the one named last changes fastest.
Arguments:
- tokens: bfloat16 [2, 2048, 1152], P(None, ('seq', 'wide')), may hold values from -6 to 6
- out_grad: bfloat16 [2, 2048, 1152], P(None, ('seq', 'wide')), may hold values from -6 to 6
- norm_attn: bfloat16 [1152], P(('seq', 'wide')), may hold values from 0.25 to 1.75
- w_query: bfloat16 [1152, 1024], P(('seq', 'wide')), may hold values from -0.1875 to 0.1875
- w_key: bfloat16 [1152, 256], P(('seq', 'wide')), may hold values from -0.1875 to 0.1875
- w_value: bfloat16 [1152, 256], P(('seq', 'wide')), may hold values from -0.1875 to 0.1875
- norm_query: bfloat16 [256], P(('seq', 'wide')), may hold values from 0.25 to 1.75
- norm_key: bfloat16 [256], P(('seq', 'wide')), may hold values from 0.25 to 1.75
- w_output: bfloat16 [1024, 1152], P(('seq', 'wide')), may hold values from -0.1875 to 0.1875
- norm_attn_post: bfloat16 [1152], P(('seq', 'wide')), may hold values from 0.25 to 1.75
- norm_ffw: bfloat16 [1152], P(('seq', 'wide')), may hold values from 0.25 to 1.75
- w_gate: bfloat16 [1152, 6912], P(('seq', 'wide')), may hold values from -0.1875 to 0.1875
- w_up: bfloat16 [1152, 6912], P(('seq', 'wide')), may hold values from -0.1875 to 0.1875
- w_down: bfloat16 [6912, 1152], P(('seq', 'wide')), may hold values from -0.078125 to 0.078125
- norm_ffw_post: bfloat16 [1152], P(('seq', 'wide')), may hold values from 0.25 to 1.75
Outputs:
- layer_out: bfloat16 [2, 2048, 1152], P(None, ('seq', 'wide'))
- input_grad: float32 [2, 2048, 1152], P(None, ('seq', 'wide'))
- grad_norm_attn: float32 [1152], P(('seq', 'wide'))
- grad_w_query: float32 [1152, 1024], P(('seq', 'wide'))
- grad_w_key: float32 [1152, 256], P(('seq', 'wide'))
- grad_w_value: float32 [1152, 256], P(('seq', 'wide'))
- grad_norm_query: float32 [256], P(('seq', 'wide'))
- grad_norm_key: float32 [256], P(('seq', 'wide'))
- grad_w_output: float32 [1024, 1152], P(('seq', 'wide'))
- grad_norm_attn_post: float32 [1152], P(('seq', 'wide'))
- grad_norm_ffw: float32 [1152], P(('seq', 'wide'))
- grad_w_gate: float32 [1152, 6912], P(('seq', 'wide'))
- grad_w_up: float32 [1152, 6912], P(('seq', 'wide'))
- grad_w_down: float32 [6912, 1152], P(('seq', 'wide'))
- grad_norm_ffw_post: float32 [1152], P(('seq', 'wide'))
The draws below stay inside these ranges and needn't reach their ends.
All inputs are finite; a program needn't handle non-finite values.
Results may differ from the reference program's by a relative error of at most 0.024.
Values may be sent and summed in bfloat16 or wider, within the bound.
A program may use at most 384 MiB of HBM per device.

```python
import math
import jax
import jax.numpy as jnp
from jax import lax

D = 1152
HEADS = 4
HEAD_DIM = 256
FF = 6912
SEQS = 2
LENGTH = 2048


def shard_levels(key, dims, cuts, low, top_value):
    def one(dim, blocks):
        steps = jax.random.uniform(jax.random.fold_in(jax.random.fold_in(key, 6), dim), (blocks,), jnp.float32, low / len(cuts), top_value / len(cuts))
        return jnp.repeat(jnp.exp(steps), dims[dim] // blocks).reshape((-1,) + (1,) * (len(dims) - dim - 1))

    gain = one(*cuts[0])
    for cut in cuts[1:]:
        gain = gain * one(*cut)
    return gain


def bell_draw(rng, dims, scale, limit, pieces=(), dtype=jnp.bfloat16):
    drawn = scale * jax.random.normal(rng, dims, jnp.float32)
    if pieces:
        drawn = drawn * shard_levels(rng, dims, pieces, -0.22, 0.18)
    return jnp.clip(drawn, -limit, limit).astype(dtype)


def setup_inputs(seed: int = 0) -> dict:
    key_list = jax.random.split(jax.random.key(seed), 16)
    tokens = bell_draw(key_list[0], (SEQS, LENGTH, D), 1.0, 6.0, ((1, 32),))
    out_grad = bell_draw(key_list[1], (SEQS, LENGTH, D), 1.0, 6.0, ((1, 32),))
    norm_attn = jnp.clip(1.0 + 0.15 * jax.random.normal(key_list[2], (D,), jnp.float32), 0.25, 1.75).astype(jnp.bfloat16)
    w_query = bell_draw(key_list[3], (D, HEADS * HEAD_DIM), D ** -0.5, 0.1875, ((0, 32),))
    w_key = bell_draw(key_list[4], (D, HEAD_DIM), D ** -0.5, 0.1875, ((0, 32),))
    w_value = bell_draw(key_list[5], (D, HEAD_DIM), D ** -0.5, 0.1875, ((0, 32),))
    norm_query = jnp.clip(1.0 + 0.15 * jax.random.normal(key_list[6], (HEAD_DIM,), jnp.float32), 0.25, 1.75).astype(jnp.bfloat16)
    norm_key = jnp.clip(1.0 + 0.15 * jax.random.normal(key_list[7], (HEAD_DIM,), jnp.float32), 0.25, 1.75).astype(jnp.bfloat16)
    w_output = bell_draw(key_list[8], (HEADS * HEAD_DIM, D), (HEADS * HEAD_DIM) ** -0.5, 0.1875, ((0, 32),))
    norm_attn_post = jnp.clip(1.0 + 0.15 * jax.random.normal(key_list[9], (D,), jnp.float32), 0.25, 1.75).astype(jnp.bfloat16)
    norm_ffw = jnp.clip(1.0 + 0.15 * jax.random.normal(key_list[10], (D,), jnp.float32), 0.25, 1.75).astype(jnp.bfloat16)
    w_gate = bell_draw(key_list[11], (D, FF), D ** -0.5, 0.1875, ((0, 32),))
    w_up = bell_draw(key_list[12], (D, FF), D ** -0.5, 0.1875, ((0, 32),))
    w_down = bell_draw(key_list[13], (FF, D), FF ** -0.5, 0.078125, ((0, 32),))
    norm_ffw_post = jnp.clip(1.0 + 0.15 * jax.random.normal(key_list[14], (D,), jnp.float32), 0.25, 1.75).astype(jnp.bfloat16)
    return {"tokens": tokens, "out_grad": out_grad, "norm_attn": norm_attn, "w_query": w_query, "w_key": w_key, "w_value": w_value, "norm_query": norm_query, "norm_key": norm_key, "w_output": w_output, "norm_attn_post": norm_attn_post, "norm_ffw": norm_ffw, "w_gate": w_gate, "w_up": w_up, "w_down": w_down, "norm_ffw_post": norm_ffw_post}


EPSILON = 1e-06
ROPE_BASE = 1000000.0
SCORE_SCALE = 0.0625
MASKED = -1e+30
HIGHEST = lax.Precision.HIGHEST

@jax.custom_vjp
def low(v):
    return lax.optimization_barrier(v.astype(jnp.bfloat16)).astype(jnp.float32)

@jax.custom_vjp
def low_back(v):
    return v

def low_keep(v):
    return (low(v), None)

def low_pass(kept, grad):
    return (grad,)

def back_keep(v):
    return (v, None)

def back_low(kept, grad):
    return (low(grad),)
low.defvjp(low_keep, low_pass)
low_back.defvjp(back_keep, back_low)

def root_norm(values, gain_vector):
    return values * lax.rsqrt(lax.optimization_barrier(jnp.mean(values * values, axis=-1, keepdims=True)) + EPSILON) * gain_vector

def rotation(positions, width):
    half_width = width // 2
    frequency = ROPE_BASE ** (-2.0 * jnp.arange(half_width).astype(jnp.float32) / width)
    angles = positions.astype(jnp.float32)[:, None] * frequency[None, :]
    return (jnp.cos(angles), jnp.sin(angles))

def rotate(values, cosine, sine_table):
    half_width = values.shape[-1] // 2
    first_half = values[..., :half_width]
    second_half = values[..., half_width:]
    return jnp.concatenate([first_half * cosine - second_half * sine_table, second_half * cosine + first_half * sine_table], axis=-1)

def product(left, right):
    return jnp.dot(left, right, precision=HIGHEST)

def layer(layer_in, weights):
    norm_attn, w_query, w_key, w_value, norm_query, norm_key, w_output, norm_attn_post, norm_ffw, w_gate, w_up, w_down, norm_ffw_post = weights
    length = layer_in.shape[0]
    positions = jnp.arange(length).astype(jnp.int32)
    cosine, sine_table = rotation(positions, HEAD_DIM)
    normed = low(root_norm(layer_in, norm_attn))
    query_raw = low_back(product(normed, w_query)).reshape(length, HEADS, HEAD_DIM)
    key_raw = low_back(product(normed, w_key))
    value_raw = low_back(product(normed, w_value))
    queries = low(rotate(root_norm(query_raw, norm_query), cosine[:, None, :], sine_table[:, None, :]))
    keys = low(rotate(root_norm(key_raw, norm_key), cosine, sine_table))
    values = low(value_raw)
    block_rows = math.gcd(length, 512)
    block_count = length // block_rows
    query_blocks = queries.reshape(block_count, block_rows, HEADS, HEAD_DIM)
    position_blocks = positions.reshape(block_count, block_rows)

    def attend(block_pair):
        query_block, query_pos = block_pair
        scores = low_back(jnp.einsum('qhd,kd->hqk', query_block, keys, precision=HIGHEST) * SCORE_SCALE)
        allowed = positions[None, None, :] <= query_pos[None, :, None]
        scores = jnp.where(allowed, scores, MASKED)
        exponent = jnp.exp(scores - lax.optimization_barrier(jnp.max(scores, axis=-1, keepdims=True)))
        probabilities = low(exponent / lax.optimization_barrier(jnp.sum(exponent, axis=-1, keepdims=True)))
        return jnp.einsum('hqk,kd->qhd', probabilities, values, precision=HIGHEST)
    attended = lax.map(jax.checkpoint(attend), (query_blocks, position_blocks))
    attended = low(low_back(attended.reshape(length, HEADS * HEAD_DIM)))
    branch = low_back(product(attended, w_output))
    mixed = layer_in + root_norm(branch, norm_attn_post)
    normed_ffw = low(root_norm(mixed, norm_ffw))
    gate = low_back(product(normed_ffw, w_gate))
    upward = low_back(product(normed_ffw, w_up))
    middle = low(jax.nn.gelu(gate, approximate=True) * upward)
    output_raw = low_back(product(middle, w_down))
    return mixed + root_norm(output_raw, norm_ffw_post)

def reference(tokens, out_grad, norm_attn, w_query, w_key, w_value, norm_query, norm_key, w_output, norm_attn_post, norm_ffw, w_gate, w_up, w_down, norm_ffw_post):
    weights = tuple((weight_arg.astype(jnp.float32) for weight_arg in (norm_attn, w_query, w_key, w_value, norm_query, norm_key, w_output, norm_attn_post, norm_ffw, w_gate, w_up, w_down, norm_ffw_post)))

    def step(totals, seq_pair):
        seq_tokens, seq_grad = seq_pair
        result, pullback = jax.vjp(layer, seq_tokens.astype(jnp.float32), weights)
        token_grad, weight_grads = pullback(seq_grad.astype(jnp.float32))
        totals = tuple((running + fresh for running, fresh in zip(totals, weight_grads)))
        return (totals, (result.astype(jnp.bfloat16), token_grad))
    zeros_start = tuple((jnp.zeros(weight_arg.shape, jnp.float32) for weight_arg in weights))
    totals, outputs = lax.scan(step, zeros_start, (tokens, out_grad))
    return (outputs[0], outputs[1], totals[0], totals[1], totals[2], totals[3], totals[4], totals[5], totals[6], totals[7], totals[8], totals[9], totals[10], totals[11], totals[12])
```

```python
import jax
import jax.numpy as jnp
from jax import lax
from jax.sharding import Mesh
from jax.sharding import PartitionSpec as P

EPSILON = 1e-06
ROPE_BASE = 1000000.0
SCORE_SCALE = 0.0625
MASKED = -1e30


def root_norm(values, gain_vector):
    return (
        values
        * lax.rsqrt(jnp.mean(values * values, axis=-1, keepdims=True) + EPSILON)
        * gain_vector
    )


def rotation(positions, width):
    half_width = width // 2
    frequency = ROPE_BASE ** (-2.0 * jnp.arange(half_width).astype(jnp.float32) / width)
    angles = positions.astype(jnp.float32)[:, None] * frequency[None, :]
    return (jnp.cos(angles), jnp.sin(angles))


def rotate(values, cosine, sine_table):
    half_width = values.shape[-1] // 2
    first_half = values[..., :half_width]
    second_half = values[..., half_width:]
    return jnp.concatenate(
        [
            first_half * cosine - second_half * sine_table,
            second_half * cosine + first_half * sine_table,
        ],
        axis=-1,
    )


def flat_norm_pull(values, gain_vector):
    return jax.vjp(root_norm, values, gain_vector)


def spread_sum(parts, axes):
    moved = lax.all_to_all(
        parts.astype(jnp.bfloat16), axes, split_axis=0, concat_axis=0, tiled=True
    )
    return jnp.sum(moved.astype(jnp.float32), axis=0)


def on_device(
    tokens,
    out_grad,
    norm_attn,
    w_query,
    w_key,
    w_value,
    norm_query,
    norm_key,
    w_output,
    norm_attn_post,
    norm_ffw,
    w_gate,
    w_up,
    w_down,
    norm_ffw_post,
):
    low = jnp.bfloat16
    full = jnp.float32
    seqs, rows, width = tokens.shape
    S = lax.axis_size("seq")
    Z = lax.axis_size("wz")
    X = lax.axis_size("wx")
    everyone = ("seq", "wz", "wx")
    group = ("seq", "wx")
    count = S * Z * X
    ranks = S * X
    heads = S
    head_dim = w_key.shape[1]
    qwidth = heads * head_dim
    wrows = w_query.shape[0]
    orows = w_output.shape[0]
    units = w_down.shape[0]
    mine = count // ranks * units
    padded = -(-mine // 128) * 128
    own = seqs * rows

    def dot(left, right):
        return jnp.dot(left, right, preferred_element_type=full)

    def dot_t(left, right):
        return jnp.einsum("nc,dc->nd", left, right, preferred_element_type=full)

    def t_dot(left, right):
        return jnp.einsum("nd,nc->dc", left, right, preferred_element_type=full)

    def column(vector):
        return jnp.pad(vector, (0, wrows - vector.shape[0]))[:, None]

    gains_own = jnp.concatenate(
        [
            column(v)
            for v in (norm_attn, norm_attn_post, norm_ffw, norm_ffw_post, norm_query, norm_key)
        ],
        axis=1,
    )
    gains_own = jnp.pad(gains_own, ((0, 0), (0, 128 - gains_own.shape[1])))
    qkv_width = qwidth + 2 * head_dim
    pack = jnp.concatenate(
        [w_query, w_key, w_value, gains_own, w_output.reshape(wrows, qwidth)], axis=1
    )
    packed = lax.all_gather(pack, everyone, axis=0, tiled=False)
    qkv_weight = packed[:, :, :qkv_width].reshape(width, qkv_width)
    output_weight = packed[:, :, qkv_width + 128 :].reshape(qwidth, width)
    gain_block = packed[:, :, qkv_width : qkv_width + 8].astype(full)
    gain_attn, gain_attn_post, gain_ffw, gain_ffw_post = (
        gain_block[:, :, i].reshape(width) for i in range(4)
    )
    gain_query, gain_key = (
        gain_block[:, : norm_query.shape[0], i].reshape(head_dim) for i in (4, 5)
    )

    def by_rank(weight):
        cut = weight.reshape(wrows, S, Z, X, units).transpose(1, 3, 0, 2, 4)
        return jnp.pad(cut.reshape(ranks, wrows, mine), ((0, 0), (0, 0), (0, padded - mine)))

    sent = jnp.concatenate([by_rank(w_gate), by_rank(w_up)], axis=2)
    arrived = lax.all_to_all(sent, group, split_axis=0, concat_axis=0, tiled=True)
    hidden_weight = lax.all_gather(
        arrived.reshape(ranks * wrows, 2 * padded), "wz", axis=0, tiled=True
    )
    down_weight = lax.all_gather(w_down, "wz", axis=0, tiled=True)

    place = jnp.arange(width, dtype=jnp.int32)
    block = place // wrows
    natural = (
        ((block // X % S) * Z + block // (S * X)) * X + block % X
    ) * wrows + place % wrows
    shuffle = (place[:, None] == natural[None, :]).astype(low)

    block_index = lax.axis_index(everyone)
    local_pos = block_index * rows + jnp.arange(rows, dtype=jnp.int32)
    cosine, sine_table = rotation(local_pos, head_dim)
    cosine = jnp.tile(cosine, (seqs, 1))
    sine_table = jnp.tile(sine_table, (seqs, 1))

    def query_side(raw_values, gain_vector):
        return rotate(
            root_norm(raw_values, gain_vector), cosine[:, None, :], sine_table[:, None, :]
        )

    def key_side(raw_values, gain_vector):
        return rotate(root_norm(raw_values, gain_vector), cosine, sine_table)

    layer_in = tokens.reshape(own, width).astype(full)
    upstream = out_grad.reshape(own, width).astype(full)
    normed_f, attn_in_pull = flat_norm_pull(layer_in, gain_attn)
    normed = normed_f.astype(low)
    qkv_raw = dot(normed, qkv_weight)
    query_raw = qkv_raw[:, :qwidth].reshape(own, heads, head_dim)
    key_raw = qkv_raw[:, qwidth : qwidth + head_dim]
    value_raw = qkv_raw[:, qwidth + head_dim :]
    key_shaped, key_pull = jax.vjp(key_side, key_raw, gain_key)
    kv_own = jnp.concatenate([key_shaped, value_raw], axis=1).astype(low)
    all_kv = lax.all_gather(
        kv_own.reshape(seqs, rows, 2 * head_dim), everyone, axis=1, tiled=True
    )
    query_shaped, query_pull = jax.vjp(query_side, query_raw, gain_query)
    queries = query_shaped.astype(low).reshape(seqs, rows * heads, head_dim)
    all_keys = all_kv[:, :, :head_dim]
    all_values = all_kv[:, :, head_dim:]
    total_len = all_kv.shape[1]
    query_pos = block_index * rows + jnp.arange(rows * heads, dtype=jnp.int32) // heads
    allowed = jnp.arange(total_len, dtype=jnp.int32)[None, :] <= query_pos[:, None]

    scores = (
        jnp.einsum("bqd,bkd->bqk", queries, all_keys, preferred_element_type=full) * SCORE_SCALE
    )
    scores = jnp.where(allowed[None], scores, MASKED)
    peak = jnp.max(scores, axis=-1, keepdims=True)
    exponent = jnp.exp(scores - peak)
    total = jnp.sum(exponent, axis=-1, keepdims=True)
    probs_f = exponent / total
    probs = probs_f.astype(low)
    attended = jnp.einsum("bqk,bkd->bqd", probs, all_values, preferred_element_type=full)
    token_heads = attended.astype(low).reshape(own, qwidth)
    branch = dot(token_heads, output_weight)
    branch_normed, attn_post_pull = flat_norm_pull(branch, gain_attn_post)
    mixed = layer_in + branch_normed
    normed_ffw_f, ffw_in_pull = flat_norm_pull(mixed, gain_ffw)
    normed_ffw = dot(normed_ffw_f.astype(low), shuffle).astype(low)

    normed_all = lax.all_gather(normed_ffw, group, axis=0, tiled=True)
    hidden = dot(normed_all, hidden_weight)
    gate = hidden[:, :padded]
    upward = hidden[:, padded:]
    middle_f, middle_pull = jax.vjp(gelu_gate, gate, upward)
    middle = middle_f.astype(low)[:, :mine]
    output_raw = spread_sum(dot(middle, down_weight).reshape(ranks, own, width), group)
    output_normed, ffw_post_pull = flat_norm_pull(output_raw, gain_ffw_post)
    layer_out = (mixed + output_normed).astype(low).reshape(tokens.shape)

    d_output_f, grad_ffw_post = ffw_post_pull(upstream)
    d_output = lax.all_gather(d_output_f.astype(low), group, axis=0, tiled=True)
    d_middle = jnp.pad(dot_t(d_output, down_weight), ((0, 0), (0, padded - mine)))
    d_gate, d_up = middle_pull(d_middle)
    d_hidden = jnp.concatenate([d_gate.astype(low), d_up.astype(low)], axis=1)
    d_shuffled = spread_sum(dot_t(d_hidden, hidden_weight).reshape(ranks, own, width), group)
    grad_down = lax.psum_scatter(
        t_dot(middle, d_output).astype(low), "wz", scatter_dimension=0, tiled=True
    ).astype(full)
    grad_hidden = lax.psum_scatter(
        t_dot(normed_all, d_hidden).astype(low), "wz", scatter_dimension=0, tiled=True
    )
    coarse = d_shuffled.astype(low)
    fine = (d_shuffled - coarse.astype(full)).astype(low)
    d_normed_ffw = dot_t(coarse, shuffle) + dot_t(fine, shuffle)
    d_mixed_part, grad_ffw = ffw_in_pull(d_normed_ffw)
    d_mixed = upstream + d_mixed_part
    d_branch_f, grad_attn_post = attn_post_pull(d_mixed)
    d_branch = d_branch_f.astype(low)
    d_attended = dot_t(d_branch, output_weight).astype(low)
    d_attended = d_attended.reshape(seqs, rows * heads, head_dim)

    d_probs = jnp.einsum("bqd,bkd->bqk", d_attended, all_values, preferred_element_type=full)
    centre = jnp.sum(probs_f * d_probs, axis=-1, keepdims=True)
    d_scores = (probs_f * (d_probs - centre)).astype(low)
    part_values = jnp.einsum("bqk,bqd->bkd", probs, d_attended, preferred_element_type=full)
    part_keys = (
        jnp.einsum("bqk,bqd->bkd", d_scores, queries, preferred_element_type=full) * SCORE_SCALE
    )
    part_kv = jnp.concatenate([part_keys.astype(low), part_values.astype(low)], axis=2)
    part_kv = part_kv.reshape(seqs, S, Z, X, rows, 2 * head_dim).transpose(1, 3, 2, 0, 4, 5)
    part_kv = spread_sum(part_kv.reshape(ranks, Z * own, 2 * head_dim), group)
    d_kv = spread_sum(part_kv.reshape(Z, own, 2 * head_dim), "wz")
    d_queries = (
        jnp.einsum("bqk,bkd->bqd", d_scores, all_keys, preferred_element_type=full) * SCORE_SCALE
    )
    d_query_raw_f, grad_query_gain = query_pull(d_queries.reshape(own, heads, head_dim))
    d_key_raw_f, grad_key_gain = key_pull(d_kv[:, :head_dim])
    d_qkv = jnp.concatenate(
        [
            d_query_raw_f.reshape(own, qwidth).astype(low),
            d_key_raw_f.astype(low),
            d_kv[:, head_dim:].astype(low),
        ],
        axis=1,
    )
    d_input_part, grad_attn = attn_in_pull(dot_t(d_qkv, qkv_weight))
    input_grad = (d_mixed + d_input_part).reshape(tokens.shape)

    def scatter(matrix, block_rows):
        columns = matrix.size // (count * block_rows)
        blocks = matrix.astype(low).reshape(S, Z, X, block_rows, columns).transpose(0, 2, 1, 3, 4)
        part = spread_sum(blocks.reshape(ranks, Z * block_rows, columns), group)
        return spread_sum(part.reshape(Z, block_rows, columns), "wz")

    out_blocks = t_dot(token_heads, d_branch).astype(low).reshape(S, Z, X, orows, width)
    out_blocks = out_blocks.transpose(0, 2, 1, 3, 4).reshape(qwidth, width)
    out_part = lax.psum_scatter(out_blocks, group, scatter_dimension=0, tiled=True)
    grad_output = lax.psum_scatter(out_part, "wz", scatter_dimension=0, tiled=True).astype(full)

    grad_qkv = scatter(t_dot(normed, d_qkv), wrows)
    grad_query_w = grad_qkv[:, :qwidth]
    grad_key_w = grad_qkv[:, qwidth : qwidth + head_dim]
    grad_value_w = grad_qkv[:, qwidth + head_dim :]

    returned = lax.all_to_all(
        grad_hidden.reshape(ranks, wrows, 2 * padded), group, split_axis=0, concat_axis=0, tiled=True
    )

    def natural_columns(part):
        cut = part[:, :, :mine].reshape(S, X, wrows, Z, units).transpose(2, 0, 3, 1, 4)
        return cut.reshape(wrows, count * units).astype(full)

    grad_gate = natural_columns(returned[:, :, :padded])
    grad_upward = natural_columns(returned[:, :, padded:])

    gain_grads = [
        grad_attn,
        grad_query_gain,
        grad_key_gain,
        grad_attn_post,
        grad_ffw,
        grad_ffw_post,
    ]
    gain_rows = jnp.concatenate([g.reshape(count, -1) for g in gain_grads], axis=1)
    gain_sums = jnp.sum(
        lax.all_to_all(gain_rows, everyone, split_axis=0, concat_axis=0, tiled=True), axis=0
    )
    gains = []
    start = 0
    for g in gain_grads:
        size = g.size // count
        gains.append(gain_sums[start : start + size])
        start += size
    return (
        layer_out,
        input_grad,
        gains[0],
        grad_query_w,
        grad_key_w,
        grad_value_w,
        gains[1],
        gains[2],
        grad_output,
        gains[3],
        gains[4],
        grad_gate,
        grad_upward,
        grad_down,
        gains[5],
    )


def gelu_gate(gate_in, up_in):
    return jax.nn.gelu(gate_in, approximate=True) * up_in


def solution(mesh):
    seq_size, wide_size = mesh.devices.shape
    mesh = Mesh(
        mesh.devices.reshape(seq_size, wide_size // 2, 2), ("seq", "wz", "wx")
    )
    placed = (
        P(None, ("seq", "wz", "wx"), None),
        P(None, ("seq", "wz", "wx"), None),
        P(("seq", "wz", "wx")),
        P(("seq", "wz", "wx"), None),
        P(("seq", "wz", "wx"), None),
        P(("seq", "wz", "wx"), None),
        P(("seq", "wz", "wx")),
        P(("seq", "wz", "wx")),
        P(("seq", "wz", "wx"), None),
        P(("seq", "wz", "wx")),
        P(("seq", "wz", "wx")),
        P(("seq", "wz", "wx"), None),
        P(("seq", "wz", "wx"), None),
        P(("seq", "wz", "wx"), None),
        P(("seq", "wz", "wx")),
    )
    return jax.shard_map(
        on_device,
        mesh=mesh,
        in_specs=placed,
        out_specs=(
            P(None, ("seq", "wz", "wx"), None),
            P(None, ("seq", "wz", "wx"), None),
            P(("seq", "wz", "wx")),
            P(("seq", "wz", "wx"), None),
            P(("seq", "wz", "wx"), None),
            P(("seq", "wz", "wx"), None),
            P(("seq", "wz", "wx")),
            P(("seq", "wz", "wx")),
            P(("seq", "wz", "wx"), None),
            P(("seq", "wz", "wx")),
            P(("seq", "wz", "wx")),
            P(("seq", "wz", "wx"), None),
            P(("seq", "wz", "wx"), None),
            P(("seq", "wz", "wx"), None),
            P(("seq", "wz", "wx")),
        ),
        check_vma=False,
    )
```

```python
import jax
import jax.numpy as jnp
from jax import lax
from jax.sharding import Mesh
from jax.sharding import PartitionSpec as P

EPSILON = 1e-06
ROPE_BASE = 1000000.0
SCORE_SCALE = 0.0625
MASKED = -1e30


def root_norm(values, gain_vector):
    return (
        values
        * lax.rsqrt(jnp.mean(values * values, axis=-1, keepdims=True) + EPSILON)
        * gain_vector
    )


def rotation(positions, width):
    half_width = width // 2
    frequency = ROPE_BASE ** (-2.0 * jnp.arange(half_width).astype(jnp.float32) / width)
    angles = positions.astype(jnp.float32)[:, None] * frequency[None, :]
    return (jnp.cos(angles), jnp.sin(angles))


def rotate(values, cosine, sine_table):
    half_width = values.shape[-1] // 2
    first_half = values[..., :half_width]
    second_half = values[..., half_width:]
    return jnp.concatenate(
        [
            first_half * cosine - second_half * sine_table,
            second_half * cosine + first_half * sine_table,
        ],
        axis=-1,
    )


def flat_norm_pull(values, gain_vector):
    return jax.vjp(root_norm, values, gain_vector)


def spread_sum(parts, axes):
    moved = lax.all_to_all(
        parts.astype(jnp.bfloat16), axes, split_axis=0, concat_axis=0, tiled=True
    )
    return jnp.sum(moved.astype(jnp.float32), axis=0)


def on_device(
    tokens,
    out_grad,
    norm_attn,
    w_query,
    w_key,
    w_value,
    norm_query,
    norm_key,
    w_output,
    norm_attn_post,
    norm_ffw,
    w_gate,
    w_up,
    w_down,
    norm_ffw_post,
):
    low = jnp.bfloat16
    full = jnp.float32
    seqs, rows, width = tokens.shape
    S = lax.axis_size("seq")
    Z = lax.axis_size("wz")
    X = lax.axis_size("wx")
    everyone = ("seq", "wz", "wx")
    group = ("seq", "wx")
    count = S * Z * X
    ranks = S * X
    heads = S
    head_dim = w_key.shape[1]
    qwidth = heads * head_dim
    wrows = w_query.shape[0]
    orows = w_output.shape[0]
    units = w_down.shape[0]
    mine = count // ranks * units
    padded = -(-mine // 128) * 128
    own = seqs * rows

    def dot(left, right):
        return jnp.dot(left, right, preferred_element_type=full)

    def dot_t(left, right):
        return jnp.einsum("nc,dc->nd", left, right, preferred_element_type=full)

    def t_dot(left, right):
        return jnp.einsum("nd,nc->dc", left, right, preferred_element_type=full)

    def column(vector):
        return jnp.pad(vector, (0, wrows - vector.shape[0]))[:, None]

    gains_own = jnp.concatenate(
        [
            column(v)
            for v in (norm_attn, norm_attn_post, norm_ffw, norm_ffw_post, norm_query, norm_key)
        ],
        axis=1,
    )
    gains_own = jnp.pad(gains_own, ((0, 0), (0, 128 - gains_own.shape[1])))
    qkv_width = qwidth + 2 * head_dim
    pack = jnp.concatenate(
        [w_query, w_key, w_value, gains_own, w_output.reshape(wrows, qwidth)], axis=1
    )
    packed = lax.all_gather(pack, everyone, axis=0, tiled=False)
    def by_rank(weight):
        cut = weight.reshape(wrows, S, Z, X, units).transpose(1, 3, 0, 2, 4)
        return jnp.pad(cut.reshape(ranks, wrows, mine), ((0, 0), (0, 0), (0, padded - mine)))

    sent = jnp.concatenate([by_rank(w_gate), by_rank(w_up)], axis=2)
    arrived = lax.all_to_all(sent, group, split_axis=0, concat_axis=0, tiled=True)
    packed, arrived = lax.optimization_barrier((packed, arrived))
    qkv_weight = packed[:, :, :qkv_width].reshape(width, qkv_width)
    output_weight = packed[:, :, qkv_width + 128 :].reshape(qwidth, width)
    gain_block = packed[:, :, qkv_width : qkv_width + 8].astype(full)
    gain_attn, gain_attn_post, gain_ffw, gain_ffw_post = (
        gain_block[:, :, i].reshape(width) for i in range(4)
    )
    gain_query, gain_key = (
        gain_block[:, : norm_query.shape[0], i].reshape(head_dim) for i in (4, 5)
    )

    hidden_weight = lax.all_gather(
        arrived.reshape(ranks * wrows, 2 * padded), "wz", axis=0, tiled=True
    )
    down_weight = lax.all_gather(w_down, "wz", axis=0, tiled=True)

    place = jnp.arange(width, dtype=jnp.int32)
    block = place // wrows
    natural = (
        ((block // X % S) * Z + block // (S * X)) * X + block % X
    ) * wrows + place % wrows
    shuffle = (place[:, None] == natural[None, :]).astype(low)

    block_index = lax.axis_index(everyone)
    local_pos = block_index * rows + jnp.arange(rows, dtype=jnp.int32)
    cosine, sine_table = rotation(local_pos, head_dim)
    cosine = jnp.tile(cosine, (seqs, 1))
    sine_table = jnp.tile(sine_table, (seqs, 1))

    def query_side(raw_values, gain_vector):
        return rotate(
            root_norm(raw_values, gain_vector), cosine[:, None, :], sine_table[:, None, :]
        )

    def key_side(raw_values, gain_vector):
        return rotate(root_norm(raw_values, gain_vector), cosine, sine_table)

    layer_in = tokens.reshape(own, width).astype(full)
    upstream = out_grad.reshape(own, width).astype(full)
    normed_f, attn_in_pull = flat_norm_pull(layer_in, gain_attn)
    normed = normed_f.astype(low)
    qkv_raw = dot(normed, qkv_weight)
    query_raw = qkv_raw[:, :qwidth].reshape(own, heads, head_dim)
    key_raw = qkv_raw[:, qwidth : qwidth + head_dim]
    value_raw = qkv_raw[:, qwidth + head_dim :]
    key_shaped, key_pull = jax.vjp(key_side, key_raw, gain_key)
    kv_own = jnp.concatenate([key_shaped, value_raw], axis=1).astype(low)
    kv_own, hidden_weight = lax.optimization_barrier((kv_own, hidden_weight))
    all_kv = lax.all_gather(
        kv_own.reshape(seqs, rows, 2 * head_dim), everyone, axis=1, tiled=True
    )
    query_shaped, query_pull = jax.vjp(query_side, query_raw, gain_query)
    queries = query_shaped.astype(low).reshape(seqs, rows * heads, head_dim)
    all_keys = all_kv[:, :, :head_dim]
    all_values = all_kv[:, :, head_dim:]
    total_len = all_kv.shape[1]
    query_pos = block_index * rows + jnp.arange(rows * heads, dtype=jnp.int32) // heads
    allowed = jnp.arange(total_len, dtype=jnp.int32)[None, :] <= query_pos[:, None]

    scores = (
        jnp.einsum("bqd,bkd->bqk", queries, all_keys, preferred_element_type=full) * SCORE_SCALE
    )
    scores = jnp.where(allowed[None], scores, MASKED)
    peak = jnp.max(scores, axis=-1, keepdims=True)
    exponent = jnp.exp(scores - peak)
    total = jnp.sum(exponent, axis=-1, keepdims=True)
    probs_f = exponent / total
    probs = probs_f.astype(low)
    attended = jnp.einsum("bqk,bkd->bqd", probs, all_values, preferred_element_type=full)
    token_heads = attended.astype(low).reshape(own, qwidth)
    branch = dot(token_heads, output_weight)
    branch_normed, attn_post_pull = flat_norm_pull(branch, gain_attn_post)
    mixed = layer_in + branch_normed
    normed_ffw_f, ffw_in_pull = flat_norm_pull(mixed, gain_ffw)
    normed_ffw = dot(normed_ffw_f.astype(low), shuffle).astype(low)

    normed_all = lax.all_gather(normed_ffw, group, axis=0, tiled=True)
    hidden = dot(normed_all, hidden_weight)
    gate = hidden[:, :padded]
    upward = hidden[:, padded:]
    middle_f, middle_pull = jax.vjp(gelu_gate, gate, upward)
    middle = middle_f.astype(low)[:, :mine]
    output_raw = spread_sum(dot(middle, down_weight).reshape(ranks, own, width), group)
    output_normed, ffw_post_pull = flat_norm_pull(output_raw, gain_ffw_post)
    layer_out = (mixed + output_normed).astype(low).reshape(tokens.shape)

    d_output_f, grad_ffw_post = ffw_post_pull(upstream)
    d_output = lax.all_gather(d_output_f.astype(low), group, axis=0, tiled=True)
    d_middle = jnp.pad(dot_t(d_output, down_weight), ((0, 0), (0, padded - mine)))
    d_gate, d_up = middle_pull(d_middle)
    d_hidden = jnp.concatenate([d_gate.astype(low), d_up.astype(low)], axis=1)
    d_shuffled = spread_sum(dot_t(d_hidden, hidden_weight).reshape(ranks, own, width), group)
    grad_hidden = lax.psum_scatter(
        t_dot(normed_all, d_hidden).astype(low), "wz", scatter_dimension=0, tiled=True
    )
    down_part = t_dot(middle, d_output).astype(low)
    down_part, grad_hidden = lax.optimization_barrier((down_part, grad_hidden))
    grad_down = lax.psum_scatter(down_part, "wz", scatter_dimension=0, tiled=True)
    coarse = d_shuffled.astype(low)
    fine = (d_shuffled - coarse.astype(full)).astype(low)
    d_normed_ffw = dot_t(coarse, shuffle) + dot_t(fine, shuffle)
    d_mixed_part, grad_ffw = ffw_in_pull(d_normed_ffw)
    d_mixed = upstream + d_mixed_part
    d_branch_f, grad_attn_post = attn_post_pull(d_mixed)
    d_branch = d_branch_f.astype(low)
    d_attended = dot_t(d_branch, output_weight).astype(low)
    d_attended = d_attended.reshape(seqs, rows * heads, head_dim)

    d_probs = jnp.einsum("bqd,bkd->bqk", d_attended, all_values, preferred_element_type=full)
    centre = jnp.sum(probs_f * d_probs, axis=-1, keepdims=True)
    d_scores = (probs_f * (d_probs - centre)).astype(low)
    part_values = jnp.einsum("bqk,bqd->bkd", probs, d_attended, preferred_element_type=full)
    part_keys = (
        jnp.einsum("bqk,bqd->bkd", d_scores, queries, preferred_element_type=full) * SCORE_SCALE
    )
    part_kv = jnp.concatenate([part_keys.astype(low), part_values.astype(low)], axis=2)
    part_kv = part_kv.reshape(seqs, S, Z, X, rows, 2 * head_dim).transpose(1, 3, 2, 0, 4, 5)
    part_kv = spread_sum(part_kv.reshape(ranks, Z * own, 2 * head_dim), group)
    d_kv = spread_sum(part_kv.reshape(Z, own, 2 * head_dim), "wz")
    d_queries = (
        jnp.einsum("bqk,bkd->bqd", d_scores, all_keys, preferred_element_type=full) * SCORE_SCALE
    )
    d_query_raw_f, grad_query_gain = query_pull(d_queries.reshape(own, heads, head_dim))
    d_key_raw_f, grad_key_gain = key_pull(d_kv[:, :head_dim])
    d_qkv = jnp.concatenate(
        [
            d_query_raw_f.reshape(own, qwidth).astype(low),
            d_key_raw_f.astype(low),
            d_kv[:, head_dim:].astype(low),
        ],
        axis=1,
    )
    d_input_part, grad_attn = attn_in_pull(dot_t(d_qkv, qkv_weight))
    input_grad = (d_mixed + d_input_part).reshape(tokens.shape)

    def scatter(matrix, block_rows):
        columns = matrix.size // (count * block_rows)
        blocks = matrix.astype(low).reshape(S, Z, X, block_rows, columns).transpose(0, 2, 1, 3, 4)
        part = spread_sum(blocks.reshape(ranks, Z * block_rows, columns), group)
        return spread_sum(part.reshape(Z, block_rows, columns), "wz")

    out_blocks = t_dot(token_heads, d_branch).astype(low).reshape(S, Z, X, orows, width)
    out_blocks = out_blocks.transpose(0, 2, 1, 3, 4).reshape(qwidth, width)
    out_blocks, grad_down = lax.optimization_barrier((out_blocks, grad_down))
    out_part = lax.psum_scatter(out_blocks, group, scatter_dimension=0, tiled=True)
    grad_output = lax.psum_scatter(out_part, "wz", scatter_dimension=0, tiled=True).astype(full)

    grad_qkv = scatter(t_dot(normed, d_qkv), wrows)
    grad_query_w = grad_qkv[:, :qwidth]
    grad_key_w = grad_qkv[:, qwidth : qwidth + head_dim]
    grad_value_w = grad_qkv[:, qwidth + head_dim :]

    returned = lax.all_to_all(
        grad_hidden.reshape(ranks, wrows, 2 * padded), group, split_axis=0, concat_axis=0, tiled=True
    )

    def natural_columns(part):
        cut = part[:, :, :mine].reshape(S, X, wrows, Z, units).transpose(2, 0, 3, 1, 4)
        return cut.reshape(wrows, count * units).astype(full)

    grad_gate = natural_columns(returned[:, :, :padded])
    grad_upward = natural_columns(returned[:, :, padded:])

    gain_grads = [
        grad_attn,
        grad_query_gain,
        grad_key_gain,
        grad_attn_post,
        grad_ffw,
        grad_ffw_post,
    ]
    gain_rows = jnp.concatenate([g.reshape(count, -1) for g in gain_grads], axis=1)
    gain_sums = jnp.sum(
        lax.all_to_all(gain_rows, everyone, split_axis=0, concat_axis=0, tiled=True), axis=0
    )
    gains = []
    start = 0
    for g in gain_grads:
        size = g.size // count
        gains.append(gain_sums[start : start + size])
        start += size
    return (
        layer_out,
        input_grad,
        gains[0],
        grad_query_w,
        grad_key_w,
        grad_value_w,
        gains[1],
        gains[2],
        grad_output,
        gains[3],
        gains[4],
        grad_gate,
        grad_upward,
        grad_down.astype(full),
        gains[5],
    )


def gelu_gate(gate_in, up_in):
    return jax.nn.gelu(gate_in, approximate=True) * up_in


def solution(mesh):
    seq_size, wide_size = mesh.devices.shape
    mesh = Mesh(
        mesh.devices.reshape(seq_size, wide_size // 2, 2), ("seq", "wz", "wx")
    )
    placed = (
        P(None, ("seq", "wz", "wx"), None),
        P(None, ("seq", "wz", "wx"), None),
        P(("seq", "wz", "wx")),
        P(("seq", "wz", "wx"), None),
        P(("seq", "wz", "wx"), None),
        P(("seq", "wz", "wx"), None),
        P(("seq", "wz", "wx")),
        P(("seq", "wz", "wx")),
        P(("seq", "wz", "wx"), None),
        P(("seq", "wz", "wx")),
        P(("seq", "wz", "wx")),
        P(("seq", "wz", "wx"), None),
        P(("seq", "wz", "wx"), None),
        P(("seq", "wz", "wx"), None),
        P(("seq", "wz", "wx")),
    )
    return jax.shard_map(
        on_device,
        mesh=mesh,
        in_specs=placed,
        out_specs=(
            P(None, ("seq", "wz", "wx"), None),
            P(None, ("seq", "wz", "wx"), None),
            P(("seq", "wz", "wx")),
            P(("seq", "wz", "wx"), None),
            P(("seq", "wz", "wx"), None),
            P(("seq", "wz", "wx"), None),
            P(("seq", "wz", "wx")),
            P(("seq", "wz", "wx")),
            P(("seq", "wz", "wx"), None),
            P(("seq", "wz", "wx")),
            P(("seq", "wz", "wx")),
            P(("seq", "wz", "wx"), None),
            P(("seq", "wz", "wx"), None),
            P(("seq", "wz", "wx"), None),
            P(("seq", "wz", "wx")),
        ),
        check_vma=False,
    )
```
